1024 devices in a mesh: dom: 128 (over z, x), grp: 8 (over y, core).
Axes of the slice: x: 4, y: 4, z: 32, core: 2. Of those that a mesh axis runs over, the one named last changes fastest.
Arguments:
- leaves: float32 [65536, 4, 128], P(('dom', 'grp')), as said below
- counts: int32 [65536], P(('dom', 'grp')), may hold values from 32 to 128, as said below
- send_list: int32 [1024, 8, 8], P(('dom', 'grp')), may hold values from 0 to 63
- pair_list: int32 [1024, 2, 128], P(('dom', 'grp')), may hold values from 0 to 63, as said below
- multipoles: float32 [35, 65536], P(None, ('dom', 'grp')), may hold values from -6 to 6
- far_list: int32 [1024, 3, 2048], P(('dom', 'grp')), may hold values from 0 to 8191, as said below
- trans_ops: float32 [35, 35, 256], replicated, may hold values from -0.1875 to 0.1875
Outputs:
- forces: float32 [65536, 3, 128], P(('dom', 'grp'))
- local_exp: float32 [35, 65536], P(None, ('dom', 'grp'))
The draws below stay inside these ranges and needn't reach their ends.
Inputs may be any that keep to these rules, and one draw needn't show every extreme that they name: `counts`: the largest count appears in every device's blocks. `pair_list`: each received slot is named by exactly two pairs of a device. `far_list`: each target cell is named by exactly 32 pairs of a device; sources lie below 8192 and classes below 256. `leaves`: positions within 0 and 1, masses positive.
All inputs are finite; a program needn't handle non-finite values.
Results may differ from the reference program's by a relative error of at most 0.000076.
Values sent between devices are 32-bit elements; how exact they have to be, the bound alone decides.
No kernel may reach another device: no remote copies, remote signals or barrier semaphores. Data moves between devices by JAX's collectives and lax.ppermute only.
A program may use at most 64 MiB of HBM per device.

```python
import jax
import jax.numpy as jnp
from jax import lax

NCOEF = 35
CLASSES = 256
LEAF_DEV = 64
SEND_SLOTS = 8
CELLS_DEV = 64
FAR_DEV = 2048
PAIRS_PER_DEVICE = 128
LEAVES = 65536
CELLS = 65536
N_DOM = 128
N_GRP = 8
DEVICES = 1024


def shuffled(key, rows, length):
    scores = jax.random.randint(key, (rows, length), 0, 2 ** 18) * length + jnp.arange(length, dtype=jnp.int32)[None, :]
    return jnp.argsort(scores, axis=1).astype(jnp.int32)


def draw_leaves(key, part):
    key = jax.random.fold_in(key, 1)
    key_pos, key_mass = jax.random.split(key)
    spots = jax.random.uniform(key_pos, (LEAVES, 3, 128), jnp.float32)
    logs = jax.random.uniform(key_mass, (LEAVES, 1, 128), jnp.float32, jnp.log(0.002), jnp.log(0.02))
    return jnp.concatenate([spots, jnp.exp(logs)], axis=1)


def draw_counts(key, part):
    key = jax.random.fold_in(key, 2)
    values = jax.random.randint(key, (LEAVES,), 32, 129)
    values = values.at[0::LEAF_DEV].set(128)
    values = values.at[1::LEAF_DEV].set(32)
    return values.astype(jnp.int32)


def draw_send_list(key, part):
    key = jax.random.fold_in(key, 3)
    values = jax.random.randint(key, (DEVICES, N_GRP, SEND_SLOTS), 0, LEAF_DEV)
    values = values.at[:, 0, 0].set(LEAF_DEV - 1)
    values = values.at[:, N_GRP - 1, SEND_SLOTS - 1].set(0)
    return values.astype(jnp.int32)


def draw_pair_list(key, part):
    key = jax.random.fold_in(key, 4)
    key_leaf, key_slot = jax.random.split(key)
    leaf = jax.random.randint(key_leaf, (DEVICES, PAIRS_PER_DEVICE), 0, LEAF_DEV)
    leaf = leaf.at[:, 0].set(LEAF_DEV - 1)
    leaf = leaf.at[:, 1].set(0)
    slot = shuffled(key_slot, DEVICES, PAIRS_PER_DEVICE) % (N_GRP * SEND_SLOTS)
    return jnp.stack([leaf.astype(jnp.int32), slot], axis=1)


def draw_far_list(key, part):
    key = jax.random.fold_in(key, 5)
    key_tgt, key_src, key_cls = jax.random.split(key, 3)
    target = shuffled(key_tgt, DEVICES, FAR_DEV) % CELLS_DEV
    source = jax.random.randint(key_src, (DEVICES, FAR_DEV), 0, N_DOM * CELLS_DEV)
    source = source.at[:, 0].set(N_DOM * CELLS_DEV - 1)
    source = source.at[:, 1].set(0)
    klass = jax.random.randint(key_cls, (DEVICES, FAR_DEV), 0, CLASSES)
    klass = klass.at[:, 0].set(CLASSES - 1)
    klass = klass.at[:, 1].set(0)
    return jnp.stack([target, source.astype(jnp.int32), klass.astype(jnp.int32)], axis=1)


def steps_of(key, dims, cuts, low, largest):
    gain, own = 1.0, jax.random.fold_in(key, 6)
    for dim, parts in cuts:
        draws = jnp.exp(jax.random.uniform(jax.random.fold_in(own, dim), (parts,), jnp.float32, low / len(cuts), largest / len(cuts)))
        gain = gain * jnp.repeat(draws, dims[dim] // parts).reshape([-1 if axis == dim else 1 for axis in range(len(dims))])
    return gain


def scatter_about(own_key, shape, scale, reach, cuts=(), kind=jnp.bfloat16):
    result = scale * jax.random.normal(own_key, shape, jnp.float32)
    if cuts:
        result = result * steps_of(own_key, shape, cuts, -0.22, 0.18)
    return jnp.clip(result, -reach, reach).astype(kind)


def setup_inputs(seed: int = 0) -> dict:
    keys = jax.random.split(jax.random.key(seed), 8)
    return {
        "leaves": draw_leaves(jax.random.fold_in(keys[7], 71), 0),
        "counts": draw_counts(jax.random.fold_in(keys[7], 71), 0),
        "send_list": draw_send_list(jax.random.fold_in(keys[7], 71), 0),
        "pair_list": draw_pair_list(jax.random.fold_in(keys[7], 71), 0),
        "multipoles": scatter_about(keys[4], (NCOEF, CELLS), 1.0, 6.0, ((1, 1024),), jnp.float32),
        "far_list": draw_far_list(jax.random.fold_in(keys[7], 71), 0),
        "trans_ops": scatter_about(keys[6], (NCOEF, NCOEF, CLASSES), (NCOEF * FAR_DEV // CELLS_DEV) ** -0.5, 0.1875, (), jnp.float32),
    }


SOFTEN = 0.04


def pair_forces(block_a, block_b):
    delta = block_b[:, :3, None, :] - block_a[:, :3, :, None]
    dist = jnp.sum(delta * delta, axis=1) + SOFTEN
    weight = dist ** -1.5
    force_a = jnp.sum(delta * (block_b[:, 3, None, :] * weight)[:, None], axis=3)
    second_force = -jnp.sum(delta * (block_a[:, 3, :, None] * weight)[:, None], axis=2)
    return force_a, second_force


def reference(leaves, counts, send_list, pair_list, multipoles, far_list, trans_ops):
    block_width = leaves.shape[2]
    live = (jnp.arange(block_width, dtype=jnp.int32)[None, :] < counts[:, None]).astype(jnp.float32)
    masked = jnp.concatenate([leaves[:, :3], leaves[:, 3:4] * live[:, None, :]], axis=1)
    masked_r = masked.reshape(N_DOM, N_GRP, LEAF_DEV, 4, block_width)
    send_r = send_list.reshape(N_DOM, N_GRP, N_GRP, SEND_SLOTS)
    pairs_r = pair_list.reshape(N_DOM, N_GRP, 2, PAIRS_PER_DEVICE)
    number_slots = N_GRP * SEND_SLOTS

    def near_dom(adom):
        def near_one(gidx):
            table = send_r[adom, :, gidx, :]
            received_blocks = masked_r[adom][jnp.arange(N_GRP, dtype=jnp.int32)[:, None], table]
            received_blocks = received_blocks.reshape(number_slots, 4, block_width)
            leaf_idx = pairs_r[adom, gidx, 0]
            slot_index = pairs_r[adom, gidx, 1]
            force_a, second_force = pair_forces(masked_r[adom, gidx][leaf_idx], received_blocks[slot_index])
            own = jnp.zeros((LEAF_DEV, 3 * block_width), jnp.float32).at[leaf_idx].add(force_a.reshape(PAIRS_PER_DEVICE, -1))
            force_per_slot = jnp.zeros((number_slots, 3 * block_width), jnp.float32).at[slot_index].add(second_force.reshape(PAIRS_PER_DEVICE, -1))
            return own, force_per_slot.reshape(N_GRP, SEND_SLOTS, 3 * block_width)
        return lax.map(near_one, jnp.arange(N_GRP, dtype=jnp.int32))

    own, force_per_slot = lax.map(near_dom, jnp.arange(N_DOM, dtype=jnp.int32))
    returned_forces = jnp.swapaxes(force_per_slot, 1, 2)

    def add_back(own_one, ret_one, table):
        return own_one.at[table.reshape(-1)].add(ret_one.reshape(-1, 3 * block_width))

    total = jax.vmap(jax.vmap(add_back))(own, returned_forces, send_r)
    forces = total.reshape(N_DOM * N_GRP * LEAF_DEV, 3, block_width) * live[:, None, :]

    multi_r = multipoles.reshape(NCOEF, N_DOM, N_GRP, CELLS_DEV)
    far_r = far_list.reshape(N_DOM, N_GRP, 3, FAR_DEV)

    def far_dom(adom):
        def far_one(gidx):
            entries = far_r[adom, gidx]
            column = multi_r[:, :, gidx, :].reshape(NCOEF, N_DOM * CELLS_DEV)
            picked = column[:, entries[1]]
            ops = trans_ops[:, :, entries[2]]
            translated = jnp.einsum("jkp,kp->pj", ops, picked, precision=lax.Precision.HIGHEST)
            local = jnp.zeros((CELLS_DEV, NCOEF), jnp.float32).at[entries[0]].add(translated)
            return local.T
        return lax.map(far_one, jnp.arange(N_GRP, dtype=jnp.int32))

    local_all = lax.map(far_dom, jnp.arange(N_DOM, dtype=jnp.int32))
    local_exp = jnp.transpose(local_all, (2, 0, 1, 3)).reshape(NCOEF, N_DOM * N_GRP * CELLS_DEV)
    return forces, local_exp
```

```python
import jax
import jax.numpy as jnp
from jax import lax
from jax.experimental import pallas as pl
from jax.experimental.pallas import tpu as pltpu
from jax.sharding import Mesh, PartitionSpec as P

SOFTEN = 0.04
F32 = jnp.float32
BF16 = jnp.bfloat16
NCOEF = 35
STRIDE = 40
NGROUP = 48
TILE = 64
NTILE = 80
ROWS = NTILE * TILE
CHUNK = 8
BATCH = 8
MOVES = 32
NFAR = 2048
LEAF = 64
PAIRS = 128
TABLE = 8192

VMEM = pl.BlockSpec(memory_space=pltpu.VMEM)
SMEM = pl.BlockSpec(memory_space=pltpu.SMEM)
ANY = pl.BlockSpec(memory_space=pl.ANY)


def params(mb=32):
    return pltpu.CompilerParams(vmem_limit_bytes=mb * 2**20)


def lanes(shape):
    return lax.broadcasted_iota(jnp.int32, shape, len(shape) - 1)


def rows(shape):
    return lax.broadcasted_iota(jnp.int32, shape, len(shape) - 2)


def pack_kernel(leaves, counts, send, out):
    lane, row = lanes((4, 128)), rows((4, 128))

    def step(k, _):
        l = send[k]
        dead = (row == 3) & (lane >= counts[l])
        out[k] = jnp.where(dead, 0.0, leaves[l])
        return 0

    lax.fori_loop(0, LEAF, step, 0, unroll=8)


def split(x):
    h = x.astype(BF16)
    r = x - h.astype(F32)
    m = r.astype(BF16)
    return h, m, (r - m.astype(F32)).astype(BF16)


def split_rows(x):
    return [p.astype(F32) for p in split(x)]


def pair_kernel(pairs, counts, leaves, received, own, slot, a_dist, b_dist, a_sums, b_sums, a_pos, b_pos, a_cen, b_cen,
                filled, named):
    lane, row = lanes((4, 128)), rows((4, 128))
    one, zero = jnp.ones((1, 128), F32), jnp.zeros((3, 128), F32)
    own[...] = jnp.zeros_like(own)

    def sums_of(block):
        pos, mass = block[0:3], block[3:4]
        centre = jnp.broadcast_to(pos[:, 0:1], (3, 128))
        weighted = jnp.concatenate([(pos - centre) * mass, mass, one * 0.0, zero], axis=0)
        parts = split_rows(weighted)
        stacked = jnp.concatenate(parts + [jnp.zeros((8, 128), F32)], axis=0).astype(BF16)
        return stacked, jnp.concatenate([centre, one * 0.0], axis=0)

    def operands(k):
        block = jnp.where((row == 3) & (lane >= counts[k]), 0.0, leaves[k])
        pos = block[0:3]
        square = jnp.sum(pos * pos, axis=0, keepdims=True)
        h, m, l = split_rows(jnp.concatenate([-2.0 * pos, square, one, zero], axis=0))
        near = jnp.concatenate([h, h, m, h, l, m], axis=0).astype(BF16)
        other = received[k]
        pos = other[0:3]
        square = jnp.sum(pos * pos, axis=0, keepdims=True) + SOFTEN
        h, m, l = split_rows(jnp.concatenate([pos, one, square, zero], axis=0))
        far = jnp.concatenate([h, m, h, l, h, m], axis=0).T.astype(BF16)
        return near, far, sums_of(block), sums_of(other), block, other

    def prepare(c, _):
        places = [c * BATCH + j for j in range(BATCH)]
        for k, done in zip(places, [operands(k) for k in places]):
            a_dist[k], b_dist[k], (a_sums[k], a_cen[k]), (b_sums[k], b_cen[k]), a_pos[k], b_pos[k] = done
            filled[k] = 0
        return 0

    lax.fori_loop(0, LEAF // BATCH, prepare, 0)

    def invert(p, _):
        q = pairs[PAIRS + p]
        n = filled[q]
        named[2 * q + n] = pairs[p]
        filled[q] = n + 1
        return 0

    lax.fori_loop(0, PAIRS, invert, 0, unroll=4)

    def gather_sum(s):
        return (s[0:8] + s[8:16] + s[16:24])[0:4]

    back = (((1,), (1,)), ((), ()))

    gap = jnp.zeros((32, 128), BF16)

    def forces_of(q, l, n):
        near = jnp.concatenate([a_dist[l], a_dist[n]], axis=1)
        dist = jnp.dot(b_dist[q], near, preferred_element_type=F32)
        r = lax.rsqrt(dist)
        w = r * r * r
        high = w.astype(BF16)
        low = (w - high.astype(F32)).astype(BF16)
        sb = b_sums[q]
        sa = jnp.concatenate(
            [jnp.concatenate([a_sums[l], gap], axis=1), jnp.concatenate([gap, a_sums[n]], axis=1)], axis=0
        )
        fb = lax.dot_general(sa, high, back, preferred_element_type=F32)
        fb = fb + lax.dot_general(sa, low, back, preferred_element_type=F32)
        fa = jnp.dot(sb, high, preferred_element_type=F32) + jnp.dot(sb, low, preferred_element_type=F32)
        bl, bn = gather_sum(fb[0:32]), gather_sum(fb[32:64])
        fl, fn = gather_sum(fa[:, 0:128]), gather_sum(fa[:, 128:256])
        back_force = bl - (b_pos[q] - a_cen[l]) * bl[3:4] + bn - (b_pos[q] - a_cen[n]) * bn[3:4]
        centre = b_cen[q]
        return back_force, fl - (a_pos[l] - centre) * fl[3:4], fn - (a_pos[n] - centre) * fn[3:4]

    def step(c, _):
        slots = [c * BATCH + j for j in range(BATCH)]
        leaves_of = [(named[2 * q], named[2 * q + 1]) for q in slots]
        results = [forces_of(q, l, n) for q, (l, n) in zip(slots, leaves_of)]
        for q, (l, n), (fb, fl, fn) in zip(slots, leaves_of, results):
            slot[q] = fb
            own[l] += fl
            own[n] += fn
        return 0

    lax.fori_loop(0, LEAF // BATCH, step, 0)


def finish_kernel(counts, send, own, back, out, total):
    total[...] = own[...]

    def add(k, _):
        total[send[k]] += back[k]
        return 0

    lax.fori_loop(0, LEAF, add, 0, unroll=4)
    lane = lanes((3, 128))

    def mask(l, _):
        out[l] = jnp.where(lane < counts[l], total[l][0:3], 0.0)
        return 0

    lax.fori_loop(0, LEAF, mask, 0, unroll=8)


def order_kernel(far, dst_out, row_out, tile_out, rows_out):
    blocks = NFAR // 128
    klass = far[2]
    source = far[1]
    place = (klass * 1366) >> 16
    group = klass - NGROUP * place
    wave = source >> 10
    row_out[...] = (
        (((source >> 6) & 3) * 16 + ((source >> 8) & 3) * 4 + (wave >> 1)) * 128
        + (wave & 1) * 64
        + (source & 63)
    )
    sub = rows((48, 128))
    before = (rows((128, 128)) < lanes((128, 128))).astype(F32).astype(BF16)
    count = jnp.zeros((48, 1), F32)
    picks, ranks = [], []
    for b in range(blocks):
        pick = (sub == group[b : b + 1]).astype(F32)
        rank = jnp.dot(pick.astype(BF16), before, preferred_element_type=F32) + count
        count = count + jnp.sum(pick, axis=1, keepdims=True)
        picks.append(pick)
        ranks.append(rank)
    tiles = ((count.astype(jnp.int32) + (TILE - 1)) >> 6).astype(F32)
    tiles = jnp.broadcast_to(tiles, (48, 128))
    lower = (lanes((48, 48)) < rows((48, 48))).astype(F32).astype(BF16)
    start = jnp.dot(lower, tiles.astype(BF16), preferred_element_type=F32)
    done = lanes((48, 128)).astype(F32) >= start + tiles
    which = jnp.sum(done.astype(F32), axis=0, keepdims=True).astype(jnp.int32)
    which = jnp.minimum(which, NGROUP - 1)
    used = jnp.sum(tiles, axis=0, keepdims=True).astype(jnp.int32)
    which = jnp.where(lanes((1, 128)) == NTILE, used, which)
    tile_out[...] = jnp.broadcast_to(which, (8, 128))
    for b in range(blocks):
        at = jnp.sum(picks[b] * (ranks[b] + start * TILE), axis=0, keepdims=True)
        dst_out[b : b + 1] = at.astype(jnp.int32)
        hot = (rows((64, 128)) == far[0][b : b + 1]).astype(F32)
        where = jnp.broadcast_to((place[b : b + 1] + 1).astype(F32), (64, 128))
        rows_out[b * 128 : (b + 1) * 128, :] = jnp.concatenate([hot, where], axis=0).T


def spread_kernel(dst, entries, select, slots, hot):
    hot[...] = jnp.zeros_like(hot)

    def step(c, _):
        some = [c * MOVES + j for j in range(MOVES)]
        found = [(dst[f], entries[pl.ds(f, 1), :]) for f in some]
        for d, value in found:
            hot[pl.ds(d, 1), :] = value
        return 0

    lax.fori_loop(0, NFAR // MOVES, step, 0)

    def turn(b, _):
        at = pl.multiple_of(b * 128, 128)
        part = hot[pl.ds(at, 128), :]
        slots[pl.ds(at, 128), :] = jnp.where(lanes((128, 128)) < 64, pltpu.roll(part, 64, 1), part)
        select[:, pl.ds(at, 128)] = part.T[0:64].astype(BF16)
        return 0

    lax.fori_loop(0, ROWS // 128, turn, 0, unroll=4)


def stack_kernel(ops, out, stacked):
    stacked[:, 104:256, :] = jnp.zeros((NGROUP, 152, 128), F32)
    pad = jnp.zeros((STRIDE - NCOEF, 256), F32)
    tail = jnp.zeros((128 - 3 * STRIDE, 256), F32)
    for s in range(6):
        for k in range(NCOEF, STRIDE):
            stacked[:, (s // 3) * 128 + (s % 3) * STRIDE + k, :] = jnp.zeros((NGROUP, 128), F32)
    same = (rows((256, 256)) == lanes((256, 256))).astype(F32).astype(BF16)
    for first in range(0, NCOEF, 5):
        turned = []
        for k in range(first, first + 5):
            parts = []
            for p in split_rows(ops[:, k, :]):
                parts += [p, pad]
            flat = jnp.concatenate(parts + [tail], axis=0).astype(BF16)
            turned.append(lax.dot_general(same, flat, (((1,), (1,)), ((), ())), preferred_element_type=F32))
        for k in range(5):
            for s in range(6):
                size = min(NGROUP, 256 - s * NGROUP)
                at = (s // 3) * 128 + (s % 3) * STRIDE + first + k
                stacked[0:size, at, :] = turned[k][s * NGROUP : s * NGROUP + size]

    def narrow(g, _):
        out[pl.ds(g * 4, 4)] = stacked[pl.ds(g * 4, 4), 0:256].astype(BF16)
        return 0

    lax.fori_loop(0, NGROUP // 4, narrow, 0)


def far_kernel(row, dst, tile, column, ops_hbm, slots_hbm, select_hbm, out,
               ops, slots, select, table, picked, sems):
    copies = [
        pltpu.make_async_copy(ops_hbm, ops, sems.at[0]),
        pltpu.make_async_copy(slots_hbm, slots, sems.at[1]),
        pltpu.make_async_copy(select_hbm, select, sems.at[2]),
    ]
    for c in copies:
        c.start()

    pad = jnp.zeros((4, 128), F32)
    tail = jnp.zeros((8, 128), F32)

    def turn(i, _):
        turned = []
        for p in range(2):
            both = column[pl.ds(pl.multiple_of(i * 144 + p * 72, 8), 72), :]
            for h in range(2):
                one = jnp.concatenate([both[36 * h : 36 * h + 36], pad], axis=0)
                turned.append(jnp.concatenate([one, one, one, tail], axis=0).T)
        for p, value in enumerate(turned):
            table[pl.ds(pl.multiple_of((4 * i + p) * 128, 128), 128), :] = value
        return 0

    lax.fori_loop(0, 16, turn, 0)

    def pick(c, _):
        some = [c * MOVES + j for j in range(MOVES)]
        found = [(dst[f], table[pl.ds(row[f], 1), :]) for f in some]
        for d, value in found:
            picked[pl.ds(d, 1), :] = value
        return 0

    lax.fori_loop(0, NFAR // MOVES, pick, 0)
    for c in copies:
        c.wait()

    lane = lanes((TILE, 128))
    place = (lane >= STRIDE).astype(F32) + (lane >= 2 * STRIDE).astype(F32) + 1.0
    left = jnp.where(lane < 3 * STRIDE, place, -1.0)
    right = jnp.where(lane < 3 * STRIDE, place + 3.0, -1.0)

    def translate(c, total):
        at = pl.multiple_of(c * (CHUNK * TILE), CHUNK * TILE)
        out_rows = []
        for j in range(CHUNK):
            here = pl.ds(pl.multiple_of(at + j * TILE, TILE), TILE)
            x = picked[here, :]
            s = slots[here, :]
            xl = split(jnp.where(s == left, x, 0.0))
            xr = split(jnp.where(s == right, x, 0.0))
            lhs = jnp.concatenate([jnp.concatenate([a, b], axis=1) for a, b in zip(xl, xr)], axis=0)
            y = jnp.dot(lhs, ops[tile[c * CHUNK + j]], preferred_element_type=F32)
            out_rows.append(y[0:TILE] + y[TILE : 2 * TILE] + y[2 * TILE :])
        moved = split(jnp.concatenate(out_rows, axis=0))
        chosen = select[:, pl.ds(at, CHUNK * TILE)]
        for part in moved:
            total = total + jnp.dot(chosen, part, preferred_element_type=F32)
        return total

    chunks = (tile[NTILE] + CHUNK - 1) // CHUNK
    total = lax.fori_loop(0, chunks, translate, jnp.zeros((64, 128), F32))
    flat = total.T
    out[...] = flat[0:NCOEF] + flat[STRIDE : STRIDE + NCOEF] + flat[2 * STRIDE : 2 * STRIDE + NCOEF]


def stacked_ops(trans_ops):
    return pl.pallas_call(
        stack_kernel, out_shape=jax.ShapeDtypeStruct((NGROUP, 256, 128), BF16),
        in_specs=[VMEM], out_specs=VMEM, scratch_shapes=[pltpu.VMEM((NGROUP, 264, 128), F32)],
        compiler_params=params(), cost_estimate=cost(10**9, 4 * 10**6), name="stack_operators",
    )(trans_ops)


def spread_out(block, axes, n):
    return lax.all_to_all(jnp.broadcast_to(block[None], (n,) + block.shape), axes, 0, 0, tiled=True)


def first_stage(multipoles):
    block = jnp.pad(multipoles, ((0, 1), (0, 0))).reshape(9, 2, 128)
    block = spread_out(block, "u", 8)
    return block.reshape(4, 2, 36, 64).transpose(0, 2, 1, 3).reshape(4, 9, 4, 128)


def cost(flops, size):
    return pl.CostEstimate(flops=flops, bytes_accessed=size, transcendentals=0)


def near_first(leaves, counts, send):
    return pl.pallas_call(
        pack_kernel, out_shape=jax.ShapeDtypeStruct((LEAF, 4, 128), F32),
        in_specs=[VMEM, SMEM, SMEM], out_specs=VMEM, compiler_params=params(),
        cost_estimate=cost(10**6, 10**6), name="pack_blocks",
    )(leaves, counts, send)


def near_pairs(leaves, counts, pairs, received):
    return pl.pallas_call(
        pair_kernel,
        out_shape=[jax.ShapeDtypeStruct((LEAF, 4, 128), F32)] * 2,
        in_specs=[SMEM, SMEM, VMEM, VMEM], out_specs=[VMEM] * 2,
        scratch_shapes=[
            pltpu.VMEM((LEAF, 48, 128), BF16), pltpu.VMEM((LEAF, 128, 48), BF16),
            pltpu.VMEM((LEAF, 32, 128), BF16), pltpu.VMEM((LEAF, 32, 128), BF16),
            pltpu.VMEM((LEAF, 4, 128), F32), pltpu.VMEM((LEAF, 4, 128), F32),
            pltpu.VMEM((LEAF, 4, 128), F32), pltpu.VMEM((LEAF, 4, 128), F32),
            pltpu.SMEM((LEAF,), jnp.int32), pltpu.SMEM((PAIRS,), jnp.int32),
        ],
        compiler_params=params(),
        cost_estimate=cost(10**9, 4 * 10**6), name="pair_forces",
    )(pairs, counts, leaves, received)


def near_last(counts, send, own, back):
    return pl.pallas_call(
        finish_kernel, out_shape=jax.ShapeDtypeStruct((LEAF, 3, 128), F32),
        in_specs=[SMEM, SMEM, VMEM, VMEM], out_specs=VMEM,
        scratch_shapes=[pltpu.VMEM((LEAF, 4, 128), F32)], compiler_params=params(),
        cost_estimate=cost(10**6, 10**6), name="add_returned",
    )(counts, send, own, back)


def far_order(far):
    dst, row, tile, entries = pl.pallas_call(
        order_kernel,
        out_shape=[jax.ShapeDtypeStruct((16, 128), jnp.int32), jax.ShapeDtypeStruct((16, 128), jnp.int32),
                   jax.ShapeDtypeStruct((8, 128), jnp.int32), jax.ShapeDtypeStruct((NFAR, 128), F32)],
        in_specs=[VMEM], out_specs=[VMEM] * 4, compiler_params=params(),
        cost_estimate=cost(10**8, 10**5), name="class_order",
    )(far.reshape(3, 16, 128))
    dst = dst.reshape(NFAR)
    select, slots = pl.pallas_call(
        spread_kernel,
        out_shape=[jax.ShapeDtypeStruct((64, ROWS), BF16), jax.ShapeDtypeStruct((ROWS, 128), F32)],
        in_specs=[SMEM, VMEM], out_specs=[VMEM] * 2,
        scratch_shapes=[pltpu.VMEM((ROWS, 128), F32)], compiler_params=params(),
        cost_estimate=cost(10**9, 4 * 10**6), name="sorted_targets",
    )(dst, entries)
    return dst, row.reshape(NFAR), tile[0], select, slots


def far_last(dst, row, tile, select, slots, ops, column):
    return pl.pallas_call(
        far_kernel, out_shape=jax.ShapeDtypeStruct((NCOEF, 64), F32),
        in_specs=[SMEM, SMEM, SMEM, VMEM, ANY, ANY, ANY], out_specs=VMEM,
        scratch_shapes=[
            pltpu.VMEM((NGROUP, 256, 128), BF16), pltpu.VMEM((ROWS, 128), F32), pltpu.VMEM((64, ROWS), BF16),
            pltpu.VMEM((TABLE, 128), F32), pltpu.VMEM((ROWS, 128), F32),
            pltpu.SemaphoreType.DMA((3,)),
        ],
        compiler_params=params(40), cost_estimate=cost(10**9, 8 * 10**6), name="translate",
    )(row, dst, tile, column, ops, slots, select)


def shards(leaves, counts, send_list, pair_list, multipoles, far_list, trans_ops):
    send = send_list.reshape(64)
    outgoing = near_first(leaves, counts, send).reshape(8, 8, 4, 128)
    received = lax.all_to_all(outgoing, "grp", 0, 0, tiled=True).reshape(64, 4, 128)
    own, slot = near_pairs(leaves, counts, pair_list.reshape(2 * PAIRS), received)
    back = lax.all_to_all(slot.reshape(8, 8, 4, 128), "grp", 0, 0, tiled=True).reshape(64, 4, 128)
    forces = near_last(counts, send, own, back)
    block = first_stage(multipoles)
    block, far_list = lax.optimization_barrier((block, far_list))
    block = spread_out(block, "v", 4).reshape(16, 9, 4, 128)
    dst, row, tile, select, slots = far_order(far_list[0])
    block, trans_ops, slots, select = lax.optimization_barrier((block, trans_ops, slots, select))
    block = spread_out(block, "x", 4)
    ops = stacked_ops(trans_ops)
    local = far_last(dst, row, tile, select, slots, ops, block.reshape(64 * 36, 128))
    return forces, local


def solution(mesh):
    fine = Mesh(mesh.devices.reshape(8, 4, 4, 8), ("u", "v", "x", "grp"))
    every = ("u", "v", "x", "grp")
    return jax.shard_map(
        shards,
        mesh=fine,
        in_specs=(P(every, None, None), P(every), P(every, None, None), P(every, None, None),
                  P(None, every), P(every, None, None), P()),
        out_specs=(P(every, None, None), P(None, every)),
        check_vma=False,
    )
```

```python
import jax
import jax.numpy as jnp
from jax import lax
from jax.experimental import pallas as pl
from jax.experimental.pallas import tpu as pltpu
from jax.sharding import Mesh, PartitionSpec as P

SOFTEN = 0.04
F32 = jnp.float32
BF16 = jnp.bfloat16
NCOEF = 35
STRIDE = 40
NGROUP = 48
TILE = 64
NTILE = 80
ROWS = NTILE * TILE
CHUNK = 16
BATCH = 16
MOVES = 64
NFAR = 2048
LEAF = 64
PAIRS = 128
TABLE = 8192

VMEM = pl.BlockSpec(memory_space=pltpu.VMEM)
SMEM = pl.BlockSpec(memory_space=pltpu.SMEM)
ANY = pl.BlockSpec(memory_space=pl.ANY)


def params(mb=16):
    return pltpu.CompilerParams(vmem_limit_bytes=mb * 2**20)


def lanes(shape):
    return lax.broadcasted_iota(jnp.int32, shape, len(shape) - 1)


def rows(shape):
    return lax.broadcasted_iota(jnp.int32, shape, len(shape) - 2)


def pack_kernel(leaves, counts, send, out):
    lane, row = lanes((4, 128)), rows((4, 128))

    def step(k, _):
        l = send[k]
        dead = (row == 3) & (lane >= counts[l])
        out[k] = jnp.where(dead, 0.0, leaves[l])
        return 0

    lax.fori_loop(0, LEAF, step, 0, unroll=8)


def split(x):
    h = x.astype(BF16)
    r = x - h.astype(F32)
    m = r.astype(BF16)
    return h, m, (r - m.astype(F32)).astype(BF16)


def split_rows(x):
    return [p.astype(F32) for p in split(x)]


def pair_kernel(pairs, counts, leaves, received, own, slot, a_dist, b_dist, a_sums, b_sums, a_pos, b_pos, a_cen, b_cen,
                filled, named):
    lane, row = lanes((4, 128)), rows((4, 128))
    one, zero = jnp.ones((1, 128), F32), jnp.zeros((3, 128), F32)
    own[...] = jnp.zeros_like(own)

    def sums_of(block):
        pos, mass = block[0:3], block[3:4]
        centre = jnp.broadcast_to(pos[:, 0:1], (3, 128))
        weighted = jnp.concatenate([(pos - centre) * mass, mass, one * 0.0, zero], axis=0)
        parts = split_rows(weighted)
        stacked = jnp.concatenate(parts + [jnp.zeros((8, 128), F32)], axis=0).astype(BF16)
        return stacked, jnp.concatenate([centre, one * 0.0], axis=0)

    def operands(k):
        block = jnp.where((row == 3) & (lane >= counts[k]), 0.0, leaves[k])
        pos = block[0:3]
        square = jnp.sum(pos * pos, axis=0, keepdims=True)
        h, m, l = split_rows(jnp.concatenate([-2.0 * pos, square, one, zero], axis=0))
        near = jnp.concatenate([h, h, m, h, l, m], axis=0).astype(BF16)
        other = received[k]
        pos = other[0:3]
        square = jnp.sum(pos * pos, axis=0, keepdims=True) + SOFTEN
        h, m, l = split_rows(jnp.concatenate([pos, one, square, zero], axis=0))
        far = jnp.concatenate([h, m, h, l, h, m], axis=0).T.astype(BF16)
        return near, far, sums_of(block), sums_of(other), block, other

    def prepare(c, _):
        places = [c * BATCH + j for j in range(BATCH)]
        for k, done in zip(places, [operands(k) for k in places]):
            a_dist[k], b_dist[k], (a_sums[k], a_cen[k]), (b_sums[k], b_cen[k]), a_pos[k], b_pos[k] = done
            filled[k] = 0
        return 0

    lax.fori_loop(0, LEAF // BATCH, prepare, 0)

    def invert(p, _):
        q = pairs[PAIRS + p]
        n = filled[q]
        named[2 * q + n] = pairs[p]
        filled[q] = n + 1
        return 0

    lax.fori_loop(0, PAIRS, invert, 0, unroll=4)

    def gather_sum(s):
        return (s[0:8] + s[8:16] + s[16:24])[0:4]

    back = (((1,), (1,)), ((), ()))

    gap = jnp.zeros((32, 128), BF16)

    def weights(dist):
        r = lax.rsqrt(dist)
        w = r * r * r
        high = w.astype(BF16)
        return high, (w - high.astype(F32)).astype(BF16)

    def sums(q, l, n, high, low):
        sb = b_sums[q]
        sa = jnp.concatenate(
            [jnp.concatenate([a_sums[l], gap], axis=1), jnp.concatenate([gap, a_sums[n]], axis=1)], axis=0
        )
        fb = lax.dot_general(sa, high, back, preferred_element_type=F32)
        fb = fb + lax.dot_general(sa, low, back, preferred_element_type=F32)
        fa = jnp.dot(sb, high, preferred_element_type=F32) + jnp.dot(sb, low, preferred_element_type=F32)
        return fa, fb

    def forces_of(q, l, n, fa, fb):
        bl, bn = gather_sum(fb[0:32]), gather_sum(fb[32:64])
        fl, fn = gather_sum(fa[:, 0:128]), gather_sum(fa[:, 128:256])
        back_force = bl - (b_pos[q] - a_cen[l]) * bl[3:4] + bn - (b_pos[q] - a_cen[n]) * bn[3:4]
        centre = b_cen[q]
        return back_force, fl - (a_pos[l] - centre) * fl[3:4], fn - (a_pos[n] - centre) * fn[3:4]

    def step(c, _):
        slots = [c * BATCH + j for j in range(BATCH)]
        named_by = [(q, named[2 * q], named[2 * q + 1]) for q in slots]
        dists = [
            jnp.dot(b_dist[q], jnp.concatenate([a_dist[l], a_dist[n]], axis=1), preferred_element_type=F32)
            for q, l, n in named_by
        ]
        parts = [weights(d) for d in dists]
        totals = [sums(*who, *part) for who, part in zip(named_by, parts)]
        results = [forces_of(*who, *total) for who, total in zip(named_by, totals)]
        for (q, l, n), (fb, fl, fn) in zip(named_by, results):
            slot[q] = fb
            own[l] += fl
            own[n] += fn
        return 0

    lax.fori_loop(0, LEAF // BATCH, step, 0)


def finish_kernel(counts, send, own, back, out, total):
    total[...] = own[...]

    def add(k, _):
        total[send[k]] += back[k]
        return 0

    lax.fori_loop(0, LEAF, add, 0, unroll=4)
    lane = lanes((3, 128))

    def mask(l, _):
        out[l] = jnp.where(lane < counts[l], total[l][0:3], 0.0)
        return 0

    lax.fori_loop(0, LEAF, mask, 0, unroll=8)


def order_kernel(far, dst_out, row_out, tile_out, rows_out):
    blocks = NFAR // 128
    klass = far[2]
    source = far[1]
    place = (klass * 1366) >> 16
    group = klass - NGROUP * place
    wave = source >> 10
    row_out[...] = (
        (((source >> 6) & 3) * 16 + ((source >> 8) & 3) * 4 + (wave >> 1)) * 128
        + (wave & 1) * 64
        + (source & 63)
    )
    sub = rows((48, 128))
    before = (rows((128, 128)) < lanes((128, 128))).astype(F32).astype(BF16)
    count = jnp.zeros((48, 1), F32)
    picks, ranks = [], []
    for b in range(blocks):
        pick = (sub == group[b : b + 1]).astype(F32)
        rank = jnp.dot(pick.astype(BF16), before, preferred_element_type=F32) + count
        count = count + jnp.sum(pick, axis=1, keepdims=True)
        picks.append(pick)
        ranks.append(rank)
    tiles = ((count.astype(jnp.int32) + (TILE - 1)) >> 6).astype(F32)
    tiles = jnp.broadcast_to(tiles, (48, 128))
    lower = (lanes((48, 48)) < rows((48, 48))).astype(F32).astype(BF16)
    start = jnp.dot(lower, tiles.astype(BF16), preferred_element_type=F32)
    done = lanes((48, 128)).astype(F32) >= start + tiles
    which = jnp.sum(done.astype(F32), axis=0, keepdims=True).astype(jnp.int32)
    which = jnp.minimum(which, NGROUP - 1)
    used = jnp.sum(tiles, axis=0, keepdims=True).astype(jnp.int32)
    which = jnp.where(lanes((1, 128)) == NTILE, used, which)
    tile_out[...] = jnp.broadcast_to(which, (8, 128))
    for b in range(blocks):
        at = jnp.sum(picks[b] * (ranks[b] + start * TILE), axis=0, keepdims=True)
        dst_out[b : b + 1] = at.astype(jnp.int32)
        hot = (rows((64, 128)) == far[0][b : b + 1]).astype(F32)
        where = jnp.broadcast_to((place[b : b + 1] + 1).astype(F32), (64, 128))
        rows_out[b * 128 : (b + 1) * 128, :] = jnp.concatenate([hot, where], axis=0).T


def spread_kernel(dst, entries, sorted_out, hot):
    hot[...] = jnp.zeros_like(hot)

    def step(c, _):
        some = [c * MOVES + j for j in range(MOVES)]
        found = [(dst[f], entries[pl.ds(f, 1), :]) for f in some]
        for d, value in found:
            hot[pl.ds(d, 1), :] = value
        return 0

    lax.fori_loop(0, NFAR // MOVES, step, 0)

    def turn(b, _):
        at = pl.multiple_of(b * 128, 128)
        part = hot[pl.ds(at, 128), :]
        spread = jnp.where(lanes((128, 128)) < 64, pltpu.roll(part, 64, 1), part)
        sorted_out[pl.ds(at, 128), :] = spread.astype(BF16)
        sorted_out[pl.ds(pl.multiple_of(ROWS + b * 64, 64), 64), :] = part.T[0:64].astype(BF16)
        return 0

    lax.fori_loop(0, ROWS // 128, turn, 0, unroll=4)


def stack_kernel(ops, out, stacked):
    stacked[:, 104:256, :] = jnp.zeros((NGROUP, 152, 128), F32)
    pad = jnp.zeros((STRIDE - NCOEF, 256), F32)
    tail = jnp.zeros((128 - 3 * STRIDE, 256), F32)
    for s in range(6):
        for k in range(NCOEF, STRIDE):
            stacked[:, (s // 3) * 128 + (s % 3) * STRIDE + k, :] = jnp.zeros((NGROUP, 128), F32)
    same = (rows((256, 256)) == lanes((256, 256))).astype(F32).astype(BF16)
    for first in range(0, NCOEF, 5):
        turned = []
        for k in range(first, first + 5):
            parts = []
            for p in split_rows(ops[k]):
                parts += [p, pad]
            flat = jnp.concatenate(parts + [tail], axis=0).astype(BF16)
            turned.append(lax.dot_general(same, flat, (((1,), (1,)), ((), ())), preferred_element_type=F32))
        for k in range(5):
            for s in range(6):
                size = min(NGROUP, 256 - s * NGROUP)
                at = (s // 3) * 128 + (s % 3) * STRIDE + first + k
                stacked[0:size, at, :] = turned[k][s * NGROUP : s * NGROUP + size]

    def narrow(g, _):
        out[pl.ds(g * 4, 4)] = stacked[pl.ds(g * 4, 4), 0:256].astype(BF16)
        return 0

    lax.fori_loop(0, NGROUP // 4, narrow, 0)


def far_kernel(row, dst, tile, column, ops_hbm, places_hbm, out, ops, places, table, picked, sems):
    copies = [
        pltpu.make_async_copy(ops_hbm, ops, sems.at[0]),
        pltpu.make_async_copy(places_hbm, places, sems.at[1]),
    ]
    for c in copies:
        c.start()

    pad = jnp.zeros((4, 128), F32)
    tail = jnp.zeros((8, 128), F32)

    def turn(i, _):
        turned = []
        for p in range(2):
            both = column[pl.ds(pl.multiple_of(i * 144 + p * 72, 8), 72), :]
            for h in range(2):
                one = jnp.concatenate([both[36 * h : 36 * h + 36], pad], axis=0)
                turned.append(jnp.concatenate([one, one, one, tail], axis=0).T)
        for p, value in enumerate(turned):
            table[pl.ds(pl.multiple_of((4 * i + p) * 128, 128), 128), :] = value
        return 0

    lax.fori_loop(0, 16, turn, 0)

    def pick(c, _):
        some = [c * MOVES + j for j in range(MOVES)]
        found = [(dst[f], table[pl.ds(row[f], 1), :]) for f in some]
        for d, value in found:
            picked[pl.ds(d, 1), :] = value
        return 0

    lax.fori_loop(0, NFAR // MOVES, pick, 0)
    for c in copies:
        c.wait()

    lane = lanes((TILE, 128))
    place = (lane >= STRIDE).astype(F32) + (lane >= 2 * STRIDE).astype(F32) + 1.0
    left = jnp.where(lane < 3 * STRIDE, place, -1.0)
    right = jnp.where(lane < 3 * STRIDE, place + 3.0, -1.0)

    def translate(c, total):
        at = pl.multiple_of(c * (CHUNK * TILE), CHUNK * TILE)
        lefts = []
        for j in range(CHUNK):
            here = pl.ds(pl.multiple_of(at + j * TILE, TILE), TILE)
            x = picked[here, :]
            s = places[here, :].astype(F32)
            xl = split(jnp.where(s == left, x, 0.0))
            xr = split(jnp.where(s == right, x, 0.0))
            lefts.append(jnp.concatenate([jnp.concatenate([a, b], axis=1) for a, b in zip(xl, xr)], axis=0))
        ys = [
            jnp.dot(lhs, ops[tile[c * CHUNK + j]], preferred_element_type=F32) for j, lhs in enumerate(lefts)
        ]
        moved = split(jnp.concatenate([y[0:TILE] + y[TILE : 2 * TILE] + y[2 * TILE :] for y in ys], axis=0))
        blocks = CHUNK * TILE // 128
        chosen = jnp.concatenate(
            [places[pl.ds(pl.multiple_of(ROWS + (c * blocks + b) * 64, 64), 64), :] for b in range(blocks)], axis=1
        )
        for part in moved:
            total = total + jnp.dot(chosen, part, preferred_element_type=F32)
        return total

    chunks = (tile[NTILE] + CHUNK - 1) // CHUNK
    total = lax.fori_loop(0, chunks, translate, jnp.zeros((64, 128), F32))
    flat = total.T
    out[...] = flat[0:NCOEF] + flat[STRIDE : STRIDE + NCOEF] + flat[2 * STRIDE : 2 * STRIDE + NCOEF]


def stacked_ops(trans_ops):
    return pl.pallas_call(
        stack_kernel, out_shape=jax.ShapeDtypeStruct((NGROUP, 256, 128), BF16),
        in_specs=[VMEM], out_specs=VMEM, scratch_shapes=[pltpu.VMEM((NGROUP, 264, 128), F32)],
        compiler_params=params(), cost_estimate=cost(10**9, 4 * 10**6), name="stack_operators",
    )(jnp.transpose(trans_ops, (1, 0, 2)))


def spread_out(block, axes, n):
    return lax.all_to_all(jnp.broadcast_to(block[None], (n,) + block.shape), axes, 0, 0, tiled=True)


def first_stage(multipoles):
    block = jnp.pad(multipoles, ((0, 1), (0, 0))).reshape(9, 2, 128)
    block = spread_out(block, "u", 8)
    return block.reshape(4, 2, 36, 64).transpose(0, 2, 1, 3).reshape(144, 128)


def cost(flops, size):
    return pl.CostEstimate(flops=flops, bytes_accessed=size, transcendentals=0)


def near_first(leaves, counts, send):
    return pl.pallas_call(
        pack_kernel, out_shape=jax.ShapeDtypeStruct((LEAF, 4, 128), F32),
        in_specs=[VMEM, SMEM, SMEM], out_specs=VMEM, compiler_params=params(),
        cost_estimate=cost(10**6, 10**6), name="pack_blocks",
    )(leaves, counts, send)


def near_pairs(leaves, counts, pairs, received):
    return pl.pallas_call(
        pair_kernel,
        out_shape=[jax.ShapeDtypeStruct((LEAF, 4, 128), F32)] * 2,
        in_specs=[SMEM, SMEM, VMEM, VMEM], out_specs=[VMEM] * 2,
        scratch_shapes=[
            pltpu.VMEM((LEAF, 48, 128), BF16), pltpu.VMEM((LEAF, 128, 48), BF16),
            pltpu.VMEM((LEAF, 32, 128), BF16), pltpu.VMEM((LEAF, 32, 128), BF16),
            pltpu.VMEM((LEAF, 4, 128), F32), pltpu.VMEM((LEAF, 4, 128), F32),
            pltpu.VMEM((LEAF, 4, 128), F32), pltpu.VMEM((LEAF, 4, 128), F32),
            pltpu.SMEM((LEAF,), jnp.int32), pltpu.SMEM((PAIRS,), jnp.int32),
        ],
        compiler_params=params(),
        cost_estimate=cost(10**9, 4 * 10**6), name="pair_forces",
    )(pairs, counts, leaves, received)


def near_last(counts, send, own, back):
    return pl.pallas_call(
        finish_kernel, out_shape=jax.ShapeDtypeStruct((LEAF, 3, 128), F32),
        in_specs=[SMEM, SMEM, VMEM, VMEM], out_specs=VMEM,
        scratch_shapes=[pltpu.VMEM((LEAF, 4, 128), F32)], compiler_params=params(),
        cost_estimate=cost(10**6, 10**6), name="add_returned",
    )(counts, send, own, back)


def far_order(far):
    dst, row, tile, entries = pl.pallas_call(
        order_kernel,
        out_shape=[jax.ShapeDtypeStruct((16, 128), jnp.int32), jax.ShapeDtypeStruct((16, 128), jnp.int32),
                   jax.ShapeDtypeStruct((8, 128), jnp.int32), jax.ShapeDtypeStruct((NFAR, 128), F32)],
        in_specs=[VMEM], out_specs=[VMEM] * 4, compiler_params=params(),
        cost_estimate=cost(10**8, 10**5), name="class_order",
    )(far.reshape(3, 16, 128))
    dst = dst.reshape(NFAR)
    places = pl.pallas_call(
        spread_kernel,
        out_shape=jax.ShapeDtypeStruct((ROWS + ROWS // 2, 128), BF16),
        in_specs=[SMEM, VMEM], out_specs=VMEM,
        scratch_shapes=[pltpu.VMEM((ROWS, 128), F32)], compiler_params=params(),
        cost_estimate=cost(10**9, 4 * 10**6), name="sorted_targets",
    )(dst, entries)
    return dst, row.reshape(NFAR), tile[0], places


def far_last(dst, row, tile, places, ops, column):
    return pl.pallas_call(
        far_kernel, out_shape=jax.ShapeDtypeStruct((NCOEF, 64), F32),
        in_specs=[SMEM, SMEM, SMEM, VMEM, ANY, ANY], out_specs=VMEM,
        scratch_shapes=[
            pltpu.VMEM((NGROUP, 256, 128), BF16), pltpu.VMEM((ROWS + ROWS // 2, 128), BF16),
            pltpu.VMEM((TABLE, 128), F32), pltpu.VMEM((ROWS, 128), F32),
            pltpu.SemaphoreType.DMA((2,)),
        ],
        compiler_params=params(20), cost_estimate=cost(10**9, 8 * 10**6), name="translate",
    )(row, dst, tile, column, ops, places)


def shards(leaves, counts, send_list, pair_list, multipoles, far_list, trans_ops):
    send = send_list.reshape(64)
    block = first_stage(multipoles)
    block, far_list = lax.optimization_barrier((block, far_list))
    outgoing = near_first(leaves, counts, send).reshape(8, 8, 4, 128)
    received = lax.all_to_all(outgoing, "grp", 0, 0, tiled=True).reshape(64, 4, 128)
    dst, row, tile, places = far_order(far_list[0])
    own, slot = near_pairs(leaves, counts, pair_list.reshape(2 * PAIRS), received)
    block = spread_out(block, "v", 4).reshape(576, 128)
    block, slot, trans_ops = lax.optimization_barrier((block, slot, trans_ops))
    back = lax.all_to_all(slot.reshape(8, 8, 4, 128), "grp", 0, 0, tiled=True).reshape(64, 4, 128)
    ops = stacked_ops(trans_ops)
    block, back, ops = lax.optimization_barrier((block, back, ops))
    block = spread_out(block, "x", 4)
    forces = near_last(counts, send, own, back)
    local = far_last(dst, row, tile, places, ops, block.reshape(64 * 36, 128))
    return forces, local


def solution(mesh):
    fine = Mesh(mesh.devices.reshape(8, 4, 4, 8), ("u", "v", "x", "grp"))
    every = ("u", "v", "x", "grp")
    return jax.shard_map(
        shards,
        mesh=fine,
        in_specs=(P(every, None, None), P(every), P(every, None, None), P(every, None, None),
                  P(None, every), P(every, None, None), P()),
        out_specs=(P(every, None, None), P(None, every)),
        check_vma=False,
    )
```

```python
import jax
import jax.numpy as jnp
from jax import lax
from jax.experimental import pallas as pl
from jax.experimental.pallas import tpu as pltpu
from jax.sharding import Mesh, PartitionSpec as P

SOFTEN = 0.04
F32 = jnp.float32
BF16 = jnp.bfloat16
NCOEF = 35
STRIDE = 40
NGROUP = 48
TILE = 64
NTILE = 80
ROWS = NTILE * TILE
CHUNK = 16
BATCH = 16
MOVES = 64
NFAR = 2048
LEAF = 64
PAIRS = 128
TABLE = 8192

VMEM = pl.BlockSpec(memory_space=pltpu.VMEM)
SMEM = pl.BlockSpec(memory_space=pltpu.SMEM)


def params(mb=16):
    return pltpu.CompilerParams(vmem_limit_bytes=mb * 2**20)


def lanes(shape):
    return lax.broadcasted_iota(jnp.int32, shape, len(shape) - 1)


def rows(shape):
    return lax.broadcasted_iota(jnp.int32, shape, len(shape) - 2)


def pack_kernel(leaves, counts, send, out):
    lane, row = lanes((4, 128)), rows((4, 128))

    def step(k, _):
        l = send[k]
        dead = (row == 3) & (lane >= counts[l])
        out[k] = jnp.where(dead, 0.0, leaves[l])
        return 0

    lax.fori_loop(0, LEAF, step, 0, unroll=8)


def split(x):
    h = x.astype(BF16)
    r = x - h.astype(F32)
    m = r.astype(BF16)
    return h, m, (r - m.astype(F32)).astype(BF16)


def split_rows(x):
    return [p.astype(F32) for p in split(x)]


def pair_kernel(pairs, counts, leaves, received, own, slot, a_dist, b_dist, a_sums, b_sums, a_pos, b_pos, a_cen, b_cen,
                filled, named):
    lane, row = lanes((4, 128)), rows((4, 128))
    one, zero = jnp.ones((1, 128), F32), jnp.zeros((3, 128), F32)
    own[...] = jnp.zeros_like(own)

    def sums_of(block):
        pos, mass = block[0:3], block[3:4]
        centre = jnp.broadcast_to(pos[:, 0:1], (3, 128))
        weighted = jnp.concatenate([(pos - centre) * mass, mass, one * 0.0, zero], axis=0)
        parts = split_rows(weighted)
        stacked = jnp.concatenate(parts + [jnp.zeros((8, 128), F32)], axis=0).astype(BF16)
        return stacked, jnp.concatenate([centre, one * 0.0], axis=0)

    def operands(k):
        block = jnp.where((row == 3) & (lane >= counts[k]), 0.0, leaves[k])
        pos = block[0:3]
        square = jnp.sum(pos * pos, axis=0, keepdims=True)
        h, m, l = split_rows(jnp.concatenate([-2.0 * pos, square, one, zero], axis=0))
        near = jnp.concatenate([h, h, m, h, l, m], axis=0).astype(BF16)
        other = received[k]
        pos = other[0:3]
        square = jnp.sum(pos * pos, axis=0, keepdims=True) + SOFTEN
        h, m, l = split_rows(jnp.concatenate([pos, one, square, zero], axis=0))
        far = jnp.concatenate([h, m, h, l, h, m], axis=0).T.astype(BF16)
        return near, far, sums_of(block), sums_of(other), block, other

    def prepare(c, _):
        places = [c * BATCH + j for j in range(BATCH)]
        for k, done in zip(places, [operands(k) for k in places]):
            a_dist[k], b_dist[k], (a_sums[k], a_cen[k]), (b_sums[k], b_cen[k]), a_pos[k], b_pos[k] = done
            filled[k] = 0
        return 0

    lax.fori_loop(0, LEAF // BATCH, prepare, 0)

    def invert(p, _):
        q = pairs[PAIRS + p]
        n = filled[q]
        named[2 * q + n] = pairs[p]
        filled[q] = n + 1
        return 0

    lax.fori_loop(0, PAIRS, invert, 0, unroll=4)

    def gather_sum(s):
        return (s[0:8] + s[8:16] + s[16:24])[0:4]

    back = (((1,), (1,)), ((), ()))

    gap = jnp.zeros((32, 128), BF16)

    def weights(dist):
        r = lax.rsqrt(dist)
        w = r * r * r
        high = w.astype(BF16)
        return high, (w - high.astype(F32)).astype(BF16)

    def sums(q, l, n, high, low):
        sb = b_sums[q]
        sa = jnp.concatenate(
            [jnp.concatenate([a_sums[l], gap], axis=1), jnp.concatenate([gap, a_sums[n]], axis=1)], axis=0
        )
        fb = lax.dot_general(sa, high, back, preferred_element_type=F32)
        fb = fb + lax.dot_general(sa, low, back, preferred_element_type=F32)
        fa = jnp.dot(sb, high, preferred_element_type=F32) + jnp.dot(sb, low, preferred_element_type=F32)
        return fa, fb

    def forces_of(q, l, n, fa, fb):
        bl, bn = gather_sum(fb[0:32]), gather_sum(fb[32:64])
        fl, fn = gather_sum(fa[:, 0:128]), gather_sum(fa[:, 128:256])
        back_force = bl - (b_pos[q] - a_cen[l]) * bl[3:4] + bn - (b_pos[q] - a_cen[n]) * bn[3:4]
        centre = b_cen[q]
        return back_force, fl - (a_pos[l] - centre) * fl[3:4], fn - (a_pos[n] - centre) * fn[3:4]

    def step(c, _):
        slots = [c * BATCH + j for j in range(BATCH)]
        named_by = [(q, named[2 * q], named[2 * q + 1]) for q in slots]
        dists = [
            jnp.dot(b_dist[q], jnp.concatenate([a_dist[l], a_dist[n]], axis=1), preferred_element_type=F32)
            for q, l, n in named_by
        ]
        parts = [weights(d) for d in dists]
        totals = [sums(*who, *part) for who, part in zip(named_by, parts)]
        results = [forces_of(*who, *total) for who, total in zip(named_by, totals)]
        for (q, l, n), (fb, fl, fn) in zip(named_by, results):
            slot[q] = fb
            own[l] += fl
            own[n] += fn
        return 0

    lax.fori_loop(0, LEAF // BATCH, step, 0)


def finish_kernel(counts, send, own, back, ready, out, total):
    total[...] = own[...]

    def add(k, _):
        total[send[k]] += back[k]
        return 0

    lax.fori_loop(0, LEAF, add, 0, unroll=4)
    lane = lanes((3, 128))

    def mask(l, _):
        out[l] = jnp.where(lane < counts[l], total[l][0:3], 0.0)
        return 0

    lax.fori_loop(0, LEAF, mask, 0, unroll=8)


def order_kernel(far, dst_out, row_out, tile_out, rows_out):
    blocks = NFAR // 128
    klass = far[2]
    source = far[1]
    place = (klass * 1366) >> 16
    group = klass - NGROUP * place
    wave = source >> 10
    row_out[...] = (
        (((source >> 6) & 3) * 16 + ((source >> 8) & 3) * 4 + (wave >> 1)) * 128
        + (wave & 1) * 64
        + (source & 63)
    )
    sub = rows((48, 128))
    before = (rows((128, 128)) < lanes((128, 128))).astype(F32).astype(BF16)
    count = jnp.zeros((48, 1), F32)
    picks, ranks = [], []
    for b in range(blocks):
        pick = (sub == group[b : b + 1]).astype(F32)
        rank = jnp.dot(pick.astype(BF16), before, preferred_element_type=F32) + count
        count = count + jnp.sum(pick, axis=1, keepdims=True)
        picks.append(pick)
        ranks.append(rank)
    tiles = ((count.astype(jnp.int32) + (TILE - 1)) >> 6).astype(F32)
    tiles = jnp.broadcast_to(tiles, (48, 128))
    lower = (lanes((48, 48)) < rows((48, 48))).astype(F32).astype(BF16)
    start = jnp.dot(lower, tiles.astype(BF16), preferred_element_type=F32)
    done = lanes((48, 128)).astype(F32) >= start + tiles
    which = jnp.sum(done.astype(F32), axis=0, keepdims=True).astype(jnp.int32)
    which = jnp.minimum(which, NGROUP - 1)
    used = jnp.sum(tiles, axis=0, keepdims=True).astype(jnp.int32)
    which = jnp.where(lanes((1, 128)) == NTILE, used, which)
    tile_out[...] = jnp.broadcast_to(which, (8, 128))
    for b in range(blocks):
        at = jnp.sum(picks[b] * (ranks[b] + start * TILE), axis=0, keepdims=True)
        dst_out[b : b + 1] = at.astype(jnp.int32)
        hot = (rows((64, 128)) == far[0][b : b + 1]).astype(F32)
        where = jnp.broadcast_to((place[b : b + 1] + 1).astype(F32), (64, 128))
        rows_out[b * 128 : (b + 1) * 128, :] = jnp.concatenate([hot, where], axis=0).T


def spread_kernel(dst, entries, sorted_out, ready, hot):
    hot[...] = jnp.zeros_like(hot)
    ready[...] = jnp.zeros_like(ready)

    def step(c, _):
        some = [c * MOVES + j for j in range(MOVES)]
        found = [(dst[f], entries[pl.ds(f, 1), :]) for f in some]
        for d, value in found:
            hot[pl.ds(d, 1), :] = value
        return 0

    lax.fori_loop(0, NFAR // MOVES, step, 0)

    def turn(b, _):
        at = pl.multiple_of(b * 128, 128)
        part = hot[pl.ds(at, 128), :]
        spread = jnp.where(lanes((128, 128)) < 64, pltpu.roll(part, 64, 1), part)
        sorted_out[pl.ds(at, 128), :] = spread.astype(BF16)
        sorted_out[pl.ds(pl.multiple_of(ROWS + b * 64, 64), 64), :] = part.T[0:64].astype(BF16)
        return 0

    lax.fori_loop(0, ROWS // 128, turn, 0, unroll=4)


def stack_kernel(ops, out, stacked):
    stacked[:, 104:256, :] = jnp.zeros((NGROUP, 152, 128), F32)
    pad = jnp.zeros((STRIDE - NCOEF, 256), F32)
    tail = jnp.zeros((128 - 3 * STRIDE, 256), F32)
    for s in range(6):
        for k in range(NCOEF, STRIDE):
            stacked[:, (s // 3) * 128 + (s % 3) * STRIDE + k, :] = jnp.zeros((NGROUP, 128), F32)
    same = (rows((256, 256)) == lanes((256, 256))).astype(F32).astype(BF16)
    for first in range(0, NCOEF, 5):
        turned = []
        for k in range(first, first + 5):
            parts = []
            for p in split_rows(ops[k]):
                parts += [p, pad]
            flat = jnp.concatenate(parts + [tail], axis=0).astype(BF16)
            turned.append(lax.dot_general(same, flat, (((1,), (1,)), ((), ())), preferred_element_type=F32))
        for k in range(5):
            for s in range(6):
                size = min(NGROUP, 256 - s * NGROUP)
                at = (s // 3) * 128 + (s % 3) * STRIDE + first + k
                stacked[0:size, at, :] = turned[k][s * NGROUP : s * NGROUP + size]

    def narrow(g, _):
        out[pl.ds(g * 4, 4)] = stacked[pl.ds(g * 4, 4), 0:256].astype(BF16)
        return 0

    lax.fori_loop(0, NGROUP // 4, narrow, 0)


def far_kernel(row, dst, tile, column, ops, places, out, table, picked):
    pad = jnp.zeros((4, 128), F32)
    tail = jnp.zeros((8, 128), F32)

    def turn(i, _):
        turned = []
        for p in range(2):
            both = column[pl.ds(pl.multiple_of(i * 144 + p * 72, 8), 72), :]
            for h in range(2):
                one = jnp.concatenate([both[36 * h : 36 * h + 36], pad], axis=0)
                turned.append(jnp.concatenate([one, one, one, tail], axis=0).T)
        for p, value in enumerate(turned):
            table[pl.ds(pl.multiple_of((4 * i + p) * 128, 128), 128), :] = value
        return 0

    lax.fori_loop(0, 16, turn, 0)

    def pick(c, _):
        some = [c * MOVES + j for j in range(MOVES)]
        found = [(dst[f], table[pl.ds(row[f], 1), :]) for f in some]
        for d, value in found:
            picked[pl.ds(d, 1), :] = value
        return 0

    lax.fori_loop(0, NFAR // MOVES, pick, 0)

    lane = lanes((TILE, 128))
    place = (lane >= STRIDE).astype(F32) + (lane >= 2 * STRIDE).astype(F32) + 1.0
    left = jnp.where(lane < 3 * STRIDE, place, -1.0)
    right = jnp.where(lane < 3 * STRIDE, place + 3.0, -1.0)

    def translate(c, total):
        at = pl.multiple_of(c * (CHUNK * TILE), CHUNK * TILE)
        lefts = []
        for j in range(CHUNK):
            here = pl.ds(pl.multiple_of(at + j * TILE, TILE), TILE)
            x = picked[here, :]
            s = places[here, :].astype(F32)
            xl = split(jnp.where(s == left, x, 0.0))
            xr = split(jnp.where(s == right, x, 0.0))
            lefts.append(jnp.concatenate([jnp.concatenate([a, b], axis=1) for a, b in zip(xl, xr)], axis=0))
        ys = [
            jnp.dot(lhs, ops[tile[c * CHUNK + j]], preferred_element_type=F32) for j, lhs in enumerate(lefts)
        ]
        moved = split(jnp.concatenate([y[0:TILE] + y[TILE : 2 * TILE] + y[2 * TILE :] for y in ys], axis=0))
        blocks = CHUNK * TILE // 128
        chosen = jnp.concatenate(
            [places[pl.ds(pl.multiple_of(ROWS + (c * blocks + b) * 64, 64), 64), :] for b in range(blocks)], axis=1
        )
        for part in moved:
            total = total + jnp.dot(chosen, part, preferred_element_type=F32)
        return total

    chunks = (tile[NTILE] + CHUNK - 1) // CHUNK
    total = lax.fori_loop(0, chunks, translate, jnp.zeros((64, 128), F32))
    flat = total.T
    out[...] = flat[0:NCOEF] + flat[STRIDE : STRIDE + NCOEF] + flat[2 * STRIDE : 2 * STRIDE + NCOEF]


def stacked_ops(trans_ops):
    return pl.pallas_call(
        stack_kernel, out_shape=jax.ShapeDtypeStruct((NGROUP, 256, 128), BF16),
        in_specs=[VMEM], out_specs=VMEM, scratch_shapes=[pltpu.VMEM((NGROUP, 264, 128), F32)],
        compiler_params=params(), cost_estimate=cost(10**9, 4 * 10**6), name="stack_operators",
    )(jnp.transpose(trans_ops, (1, 0, 2)))


def spread_out(block, axes, n):
    return lax.all_to_all(jnp.broadcast_to(block[None], (n,) + block.shape), axes, 0, 0, tiled=True)


def first_stage(multipoles):
    block = jnp.pad(multipoles, ((0, 1), (0, 0))).reshape(9, 2, 128)
    block = spread_out(block, "u", 8)
    return block.reshape(4, 2, 36, 64).transpose(0, 2, 1, 3).reshape(144, 128)


def cost(flops, size):
    return pl.CostEstimate(flops=flops, bytes_accessed=size, transcendentals=0)


def near_first(leaves, counts, send):
    return pl.pallas_call(
        pack_kernel, out_shape=jax.ShapeDtypeStruct((LEAF, 4, 128), F32),
        in_specs=[VMEM, SMEM, SMEM], out_specs=VMEM, compiler_params=params(),
        cost_estimate=cost(10**6, 10**6), name="pack_blocks",
    )(leaves, counts, send)


def near_pairs(leaves, counts, pairs, received):
    return pl.pallas_call(
        pair_kernel,
        out_shape=[jax.ShapeDtypeStruct((LEAF, 4, 128), F32)] * 2,
        in_specs=[SMEM, SMEM, VMEM, VMEM], out_specs=[VMEM] * 2,
        scratch_shapes=[
            pltpu.VMEM((LEAF, 48, 128), BF16), pltpu.VMEM((LEAF, 128, 48), BF16),
            pltpu.VMEM((LEAF, 32, 128), BF16), pltpu.VMEM((LEAF, 32, 128), BF16),
            pltpu.VMEM((LEAF, 4, 128), F32), pltpu.VMEM((LEAF, 4, 128), F32),
            pltpu.VMEM((LEAF, 4, 128), F32), pltpu.VMEM((LEAF, 4, 128), F32),
            pltpu.SMEM((LEAF,), jnp.int32), pltpu.SMEM((PAIRS,), jnp.int32),
        ],
        compiler_params=params(),
        cost_estimate=cost(10**9, 4 * 10**6), name="pair_forces",
    )(pairs, counts, leaves, received)


def near_last(counts, send, own, back, ready):
    return pl.pallas_call(
        finish_kernel, out_shape=jax.ShapeDtypeStruct((LEAF, 3, 128), F32),
        in_specs=[SMEM, SMEM, VMEM, VMEM, VMEM], out_specs=VMEM,
        scratch_shapes=[pltpu.VMEM((LEAF, 4, 128), F32)], compiler_params=params(),
        cost_estimate=cost(10**6, 10**6), name="add_returned",
    )(counts, send, own, back, ready)


def far_order(far):
    dst, row, tile, entries = pl.pallas_call(
        order_kernel,
        out_shape=[jax.ShapeDtypeStruct((16, 128), jnp.int32), jax.ShapeDtypeStruct((16, 128), jnp.int32),
                   jax.ShapeDtypeStruct((8, 128), jnp.int32), jax.ShapeDtypeStruct((NFAR, 128), F32)],
        in_specs=[VMEM], out_specs=[VMEM] * 4, compiler_params=params(),
        cost_estimate=cost(10**8, 10**5), name="class_order",
    )(far.reshape(3, 16, 128))
    dst = dst.reshape(NFAR)
    places, ready = pl.pallas_call(
        spread_kernel,
        out_shape=[jax.ShapeDtypeStruct((ROWS + ROWS // 2, 128), BF16), jax.ShapeDtypeStruct((8, 128), F32)],
        in_specs=[SMEM, VMEM], out_specs=[VMEM] * 2,
        scratch_shapes=[pltpu.VMEM((ROWS, 128), F32)], compiler_params=params(),
        cost_estimate=cost(10**9, 4 * 10**6), name="sorted_targets",
    )(dst, entries)
    return dst, row.reshape(NFAR), tile[0], places, ready


def far_last(dst, row, tile, places, ops, column):
    return pl.pallas_call(
        far_kernel, out_shape=jax.ShapeDtypeStruct((NCOEF, 64), F32),
        in_specs=[SMEM, SMEM, SMEM, VMEM, VMEM, VMEM], out_specs=VMEM,
        scratch_shapes=[pltpu.VMEM((TABLE, 128), F32), pltpu.VMEM((ROWS, 128), F32)],
        compiler_params=params(20), cost_estimate=cost(10**9, 8 * 10**6), name="translate",
    )(row, dst, tile, column, ops, places)


def shards(leaves, counts, send_list, pair_list, multipoles, far_list, trans_ops):
    send = send_list.reshape(64)
    block = first_stage(multipoles)
    block, far_list, trans_ops = lax.optimization_barrier((block, far_list, trans_ops))
    outgoing = near_first(leaves, counts, send).reshape(8, 8, 4, 128)
    received = lax.all_to_all(outgoing, "grp", 0, 0, tiled=True).reshape(64, 4, 128)
    ops = stacked_ops(trans_ops)
    block, received, ops = lax.optimization_barrier((block, received, ops))
    own, slot = near_pairs(leaves, counts, pair_list.reshape(2 * PAIRS), received)
    block = spread_out(block, "v", 4).reshape(576, 128)
    block, far_list, own, slot = lax.optimization_barrier((block, far_list, own, slot))
    dst, row, tile, places, ready = far_order(far_list[0])
    block = spread_out(block, "x", 4)
    block, slot, ready = lax.optimization_barrier((block, slot, ready))
    back = lax.all_to_all(slot.reshape(8, 8, 4, 128), "grp", 0, 0, tiled=True).reshape(64, 4, 128)
    local = far_last(dst, row, tile, places, ops, block.reshape(64 * 36, 128))
    forces = near_last(counts, send, own, back, ready)
    return forces, local


def solution(mesh):
    fine = Mesh(mesh.devices.reshape(8, 4, 4, 8), ("u", "v", "x", "grp"))
    every = ("u", "v", "x", "grp")
    return jax.shard_map(
        shards,
        mesh=fine,
        in_specs=(P(every, None, None), P(every), P(every, None, None), P(every, None, None),
                  P(None, every), P(every, None, None), P()),
        out_specs=(P(every, None, None), P(None, every)),
        check_vma=False,
    )
```

```python
import jax
import jax.numpy as jnp
from jax import lax
from jax.experimental import pallas as pl
from jax.experimental.pallas import tpu as pltpu
from jax.sharding import Mesh, PartitionSpec as P

SOFTEN = 0.04
F32 = jnp.float32
BF16 = jnp.bfloat16
NCOEF = 35
STRIDE = 40
NGROUP = 48
TILE = 64
NTILE = 80
ROWS = NTILE * TILE
CHUNK = 16
BATCH = 16
MOVES = 64
NFAR = 2048
LEAF = 64
PAIRS = 128
TABLE = 8192

VMEM = pl.BlockSpec(memory_space=pltpu.VMEM)
SMEM = pl.BlockSpec(memory_space=pltpu.SMEM)


def params(mb=16):
    return pltpu.CompilerParams(vmem_limit_bytes=mb * 2**20)


def lanes(shape):
    return lax.broadcasted_iota(jnp.int32, shape, len(shape) - 1)


def rows(shape):
    return lax.broadcasted_iota(jnp.int32, shape, len(shape) - 2)


def pack_kernel(leaves, counts, send, out):
    lane, row = lanes((4, 128)), rows((4, 128))

    def step(k, _):
        l = send[k]
        dead = (row == 3) & (lane >= counts[l])
        out[k] = jnp.where(dead, 0.0, leaves[l])
        return 0

    lax.fori_loop(0, LEAF, step, 0, unroll=8)


def split(x):
    h = x.astype(BF16)
    r = x - h.astype(F32)
    m = r.astype(BF16)
    return h, m, (r - m.astype(F32)).astype(BF16)


def split_rows(x):
    return [p.astype(F32) for p in split(x)]


def pair_kernel(pairs, counts, leaves, received, own, slot, a_dist, b_dist, a_sums, b_sums, a_pos, b_pos, a_cen, b_cen,
                filled, named):
    lane, row = lanes((4, 128)), rows((4, 128))
    one, zero = jnp.ones((1, 128), F32), jnp.zeros((3, 128), F32)
    own[...] = jnp.zeros_like(own)

    def sums_of(block):
        pos, mass = block[0:3], block[3:4]
        centre = jnp.broadcast_to(pos[:, 0:1], (3, 128))
        weighted = jnp.concatenate([(pos - centre) * mass, mass, one * 0.0, zero], axis=0)
        parts = split_rows(weighted)
        stacked = jnp.concatenate(parts + [jnp.zeros((8, 128), F32)], axis=0).astype(BF16)
        return stacked, jnp.concatenate([centre, one * 0.0], axis=0)

    def operands(k):
        block = jnp.where((row == 3) & (lane >= counts[k]), 0.0, leaves[k])
        pos = block[0:3]
        square = jnp.sum(pos * pos, axis=0, keepdims=True)
        h, m, l = split_rows(jnp.concatenate([-2.0 * pos, square, one, zero], axis=0))
        near = jnp.concatenate([h, h, m, h, l, m], axis=0).astype(BF16)
        other = received[k]
        pos = other[0:3]
        square = jnp.sum(pos * pos, axis=0, keepdims=True) + SOFTEN
        h, m, l = split_rows(jnp.concatenate([pos, one, square, zero], axis=0))
        far = jnp.concatenate([h, m, h, l, h, m], axis=0).T.astype(BF16)
        return near, far, sums_of(block), sums_of(other), block, other

    def prepare(c, _):
        places = [c * BATCH + j for j in range(BATCH)]
        for k, done in zip(places, [operands(k) for k in places]):
            a_dist[k], b_dist[k], (a_sums[k], a_cen[k]), (b_sums[k], b_cen[k]), a_pos[k], b_pos[k] = done
            filled[k] = 0
        return 0

    lax.fori_loop(0, LEAF // BATCH, prepare, 0)

    def invert(p, _):
        q = pairs[PAIRS + p]
        n = filled[q]
        named[2 * q + n] = pairs[p]
        filled[q] = n + 1
        return 0

    lax.fori_loop(0, PAIRS, invert, 0, unroll=4)

    def gather_sum(s):
        return (s[0:8] + s[8:16] + s[16:24])[0:4]

    back = (((1,), (1,)), ((), ()))

    gap = jnp.zeros((32, 128), BF16)

    def weights(dist):
        r = lax.rsqrt(dist)
        w = r * r * r
        high = w.astype(BF16)
        return high, (w - high.astype(F32)).astype(BF16)

    def sums(q, l, n, high, low):
        sb = b_sums[q]
        sa = jnp.concatenate(
            [jnp.concatenate([a_sums[l], gap], axis=1), jnp.concatenate([gap, a_sums[n]], axis=1)], axis=0
        )
        fb = lax.dot_general(sa, high, back, preferred_element_type=F32)
        fb = fb + lax.dot_general(sa, low, back, preferred_element_type=F32)
        fa = jnp.dot(sb, high, preferred_element_type=F32) + jnp.dot(sb, low, preferred_element_type=F32)
        return fa, fb

    def forces_of(q, l, n, fa, fb):
        bl, bn = gather_sum(fb[0:32]), gather_sum(fb[32:64])
        fl, fn = gather_sum(fa[:, 0:128]), gather_sum(fa[:, 128:256])
        back_force = bl - (b_pos[q] - a_cen[l]) * bl[3:4] + bn - (b_pos[q] - a_cen[n]) * bn[3:4]
        centre = b_cen[q]
        return back_force, fl - (a_pos[l] - centre) * fl[3:4], fn - (a_pos[n] - centre) * fn[3:4]

    def step(c, _):
        slots = [c * BATCH + j for j in range(BATCH)]
        named_by = [(q, named[2 * q], named[2 * q + 1]) for q in slots]
        dists = [
            jnp.dot(b_dist[q], jnp.concatenate([a_dist[l], a_dist[n]], axis=1), preferred_element_type=F32)
            for q, l, n in named_by
        ]
        parts = [weights(d) for d in dists]
        totals = [sums(*who, *part) for who, part in zip(named_by, parts)]
        results = [forces_of(*who, *total) for who, total in zip(named_by, totals)]
        for (q, l, n), (fb, fl, fn) in zip(named_by, results):
            slot[q] = fb
            own[l] += fl
            own[n] += fn
        return 0

    lax.fori_loop(0, LEAF // BATCH, step, 0)


def finish_kernel(counts, send, own, back, out, total):
    total[...] = own[...]

    def add(k, _):
        total[send[k]] += back[k]
        return 0

    lax.fori_loop(0, LEAF, add, 0, unroll=4)
    lane = lanes((3, 128))

    def mask(l, _):
        out[l] = jnp.where(lane < counts[l], total[l][0:3], 0.0)
        return 0

    lax.fori_loop(0, LEAF, mask, 0, unroll=8)


def order_kernel(far, dst_out, row_out, tile_out, rows_out):
    blocks = NFAR // 128
    klass = far[2]
    source = far[1]
    place = (klass * 1366) >> 16
    group = klass - NGROUP * place
    wave = source >> 10
    row_out[...] = (
        (((source >> 6) & 3) * 16 + ((source >> 8) & 3) * 4 + (wave >> 1)) * 128
        + (wave & 1) * 64
        + (source & 63)
    )
    sub = rows((48, 128))
    before = (rows((128, 128)) < lanes((128, 128))).astype(F32).astype(BF16)
    count = jnp.zeros((48, 1), F32)
    picks, ranks = [], []
    for b in range(blocks):
        pick = (sub == group[b : b + 1]).astype(F32)
        rank = jnp.dot(pick.astype(BF16), before, preferred_element_type=F32) + count
        count = count + jnp.sum(pick, axis=1, keepdims=True)
        picks.append(pick)
        ranks.append(rank)
    tiles = ((count.astype(jnp.int32) + (TILE - 1)) >> 6).astype(F32)
    tiles = jnp.broadcast_to(tiles, (48, 128))
    lower = (lanes((48, 48)) < rows((48, 48))).astype(F32).astype(BF16)
    start = jnp.dot(lower, tiles.astype(BF16), preferred_element_type=F32)
    done = lanes((48, 128)).astype(F32) >= start + tiles
    which = jnp.sum(done.astype(F32), axis=0, keepdims=True).astype(jnp.int32)
    which = jnp.minimum(which, NGROUP - 1)
    used = jnp.sum(tiles, axis=0, keepdims=True).astype(jnp.int32)
    which = jnp.where(lanes((1, 128)) == NTILE, used, which)
    tile_out[...] = jnp.broadcast_to(which, (8, 128))
    for b in range(blocks):
        at = jnp.sum(picks[b] * (ranks[b] + start * TILE), axis=0, keepdims=True)
        dst_out[b : b + 1] = at.astype(jnp.int32)
        hot = (rows((64, 128)) == far[0][b : b + 1]).astype(F32)
        where = jnp.broadcast_to((place[b : b + 1] + 1).astype(F32), (64, 128))
        rows_out[b * 128 : (b + 1) * 128, :] = jnp.concatenate([hot, where], axis=0).T


def spread_kernel(dst, entries, sorted_out, ready, hot):
    hot[...] = jnp.zeros_like(hot)
    ready[...] = jnp.zeros_like(ready)

    def step(c, _):
        some = [c * MOVES + j for j in range(MOVES)]
        found = [(dst[f], entries[pl.ds(f, 1), :]) for f in some]
        for d, value in found:
            hot[pl.ds(d, 1), :] = value
        return 0

    lax.fori_loop(0, NFAR // MOVES, step, 0)

    def turn(b, _):
        at = pl.multiple_of(b * 128, 128)
        part = hot[pl.ds(at, 128), :]
        spread = jnp.where(lanes((128, 128)) < 64, pltpu.roll(part, 64, 1), part)
        sorted_out[pl.ds(at, 128), :] = spread.astype(BF16)
        sorted_out[pl.ds(pl.multiple_of(ROWS + b * 64, 64), 64), :] = part.T[0:64].astype(BF16)
        return 0

    lax.fori_loop(0, ROWS // 128, turn, 0, unroll=4)


def stack_kernel(ops, ready, out, stacked):
    stacked[:, 104:256, :] = jnp.zeros((NGROUP, 152, 128), F32)
    pad = jnp.zeros((STRIDE - NCOEF, 256), F32)
    tail = jnp.zeros((128 - 3 * STRIDE, 256), F32)
    for s in range(6):
        for k in range(NCOEF, STRIDE):
            stacked[:, (s // 3) * 128 + (s % 3) * STRIDE + k, :] = jnp.zeros((NGROUP, 128), F32)
    same = (rows((256, 256)) == lanes((256, 256))).astype(F32).astype(BF16)
    for first in range(0, NCOEF, 5):
        turned = []
        for k in range(first, first + 5):
            parts = []
            for p in split_rows(ops[k]):
                parts += [p, pad]
            flat = jnp.concatenate(parts + [tail], axis=0).astype(BF16)
            turned.append(lax.dot_general(same, flat, (((1,), (1,)), ((), ())), preferred_element_type=F32))
        for k in range(5):
            for s in range(6):
                size = min(NGROUP, 256 - s * NGROUP)
                at = (s // 3) * 128 + (s % 3) * STRIDE + first + k
                stacked[0:size, at, :] = turned[k][s * NGROUP : s * NGROUP + size]

    def narrow(g, _):
        out[pl.ds(g * 4, 4)] = stacked[pl.ds(g * 4, 4), 0:256].astype(BF16)
        return 0

    lax.fori_loop(0, NGROUP // 4, narrow, 0)


def far_kernel(row, dst, tile, column, ops, places, out, table, picked):
    pad = jnp.zeros((4, 128), F32)
    tail = jnp.zeros((8, 128), F32)

    def turn(i, _):
        turned = []
        for p in range(2):
            both = column[pl.ds(pl.multiple_of(i * 144 + p * 72, 8), 72), :]
            for h in range(2):
                one = jnp.concatenate([both[36 * h : 36 * h + 36], pad], axis=0)
                turned.append(jnp.concatenate([one, one, one, tail], axis=0).T)
        for p, value in enumerate(turned):
            table[pl.ds(pl.multiple_of((4 * i + p) * 128, 128), 128), :] = value
        return 0

    lax.fori_loop(0, 16, turn, 0)

    def pick(c, _):
        some = [c * MOVES + j for j in range(MOVES)]
        found = [(dst[f], table[pl.ds(row[f], 1), :]) for f in some]
        for d, value in found:
            picked[pl.ds(d, 1), :] = value
        return 0

    lax.fori_loop(0, NFAR // MOVES, pick, 0)

    lane = lanes((TILE, 128))
    place = (lane >= STRIDE).astype(F32) + (lane >= 2 * STRIDE).astype(F32) + 1.0
    left = jnp.where(lane < 3 * STRIDE, place, -1.0)
    right = jnp.where(lane < 3 * STRIDE, place + 3.0, -1.0)

    def translate(c, total):
        at = pl.multiple_of(c * (CHUNK * TILE), CHUNK * TILE)
        lefts = []
        for j in range(CHUNK):
            here = pl.ds(pl.multiple_of(at + j * TILE, TILE), TILE)
            x = picked[here, :]
            s = places[here, :].astype(F32)
            xl = split(jnp.where(s == left, x, 0.0))
            xr = split(jnp.where(s == right, x, 0.0))
            lefts.append(jnp.concatenate([jnp.concatenate([a, b], axis=1) for a, b in zip(xl, xr)], axis=0))
        ys = [
            jnp.dot(lhs, ops[tile[c * CHUNK + j]], preferred_element_type=F32) for j, lhs in enumerate(lefts)
        ]
        moved = split(jnp.concatenate([y[0:TILE] + y[TILE : 2 * TILE] + y[2 * TILE :] for y in ys], axis=0))
        blocks = CHUNK * TILE // 128
        chosen = jnp.concatenate(
            [places[pl.ds(pl.multiple_of(ROWS + (c * blocks + b) * 64, 64), 64), :] for b in range(blocks)], axis=1
        )
        for part in moved:
            total = total + jnp.dot(chosen, part, preferred_element_type=F32)
        return total

    chunks = (tile[NTILE] + CHUNK - 1) // CHUNK
    total = lax.fori_loop(0, chunks, translate, jnp.zeros((64, 128), F32))
    flat = total.T
    out[...] = flat[0:NCOEF] + flat[STRIDE : STRIDE + NCOEF] + flat[2 * STRIDE : 2 * STRIDE + NCOEF]


def stacked_ops(trans_ops, ready):
    return pl.pallas_call(
        stack_kernel, out_shape=jax.ShapeDtypeStruct((NGROUP, 256, 128), BF16),
        in_specs=[VMEM] * 2, out_specs=VMEM, scratch_shapes=[pltpu.VMEM((NGROUP, 264, 128), F32)],
        compiler_params=params(), cost_estimate=cost(10**9, 4 * 10**6), name="stack_operators",
    )(jnp.transpose(trans_ops, (1, 0, 2)), ready)


def spread_out(block, axes, n):
    return lax.all_to_all(jnp.broadcast_to(block[None], (n,) + block.shape), axes, 0, 0, tiled=True)


def first_stage(multipoles):
    block = jnp.pad(multipoles, ((0, 1), (0, 0))).reshape(9, 2, 128)
    block = spread_out(block, "u", 8)
    return block.reshape(4, 2, 36, 64).transpose(0, 2, 1, 3).reshape(144, 128)


def cost(flops, size):
    return pl.CostEstimate(flops=flops, bytes_accessed=size, transcendentals=0)


def near_first(leaves, counts, send):
    return pl.pallas_call(
        pack_kernel, out_shape=jax.ShapeDtypeStruct((LEAF, 4, 128), F32),
        in_specs=[VMEM, SMEM, SMEM], out_specs=VMEM, compiler_params=params(),
        cost_estimate=cost(10**6, 10**6), name="pack_blocks",
    )(leaves, counts, send)


def near_pairs(leaves, counts, pairs, received):
    return pl.pallas_call(
        pair_kernel,
        out_shape=[jax.ShapeDtypeStruct((LEAF, 4, 128), F32)] * 2,
        in_specs=[SMEM, SMEM, VMEM, VMEM], out_specs=[VMEM] * 2,
        scratch_shapes=[
            pltpu.VMEM((LEAF, 48, 128), BF16), pltpu.VMEM((LEAF, 128, 48), BF16),
            pltpu.VMEM((LEAF, 32, 128), BF16), pltpu.VMEM((LEAF, 32, 128), BF16),
            pltpu.VMEM((LEAF, 4, 128), F32), pltpu.VMEM((LEAF, 4, 128), F32),
            pltpu.VMEM((LEAF, 4, 128), F32), pltpu.VMEM((LEAF, 4, 128), F32),
            pltpu.SMEM((LEAF,), jnp.int32), pltpu.SMEM((PAIRS,), jnp.int32),
        ],
        compiler_params=params(),
        cost_estimate=cost(10**9, 4 * 10**6), name="pair_forces",
    )(pairs, counts, leaves, received)


def near_last(counts, send, own, back):
    return pl.pallas_call(
        finish_kernel, out_shape=jax.ShapeDtypeStruct((LEAF, 3, 128), F32),
        in_specs=[SMEM, SMEM, VMEM, VMEM], out_specs=VMEM,
        scratch_shapes=[pltpu.VMEM((LEAF, 4, 128), F32)], compiler_params=params(),
        cost_estimate=cost(10**6, 10**6), name="add_returned",
    )(counts, send, own, back)


def far_order(far):
    dst, row, tile, entries = pl.pallas_call(
        order_kernel,
        out_shape=[jax.ShapeDtypeStruct((16, 128), jnp.int32), jax.ShapeDtypeStruct((16, 128), jnp.int32),
                   jax.ShapeDtypeStruct((8, 128), jnp.int32), jax.ShapeDtypeStruct((NFAR, 128), F32)],
        in_specs=[VMEM], out_specs=[VMEM] * 4, compiler_params=params(),
        cost_estimate=cost(10**8, 10**5), name="class_order",
    )(far.reshape(3, 16, 128))
    dst = dst.reshape(NFAR)
    places, ready = pl.pallas_call(
        spread_kernel,
        out_shape=[jax.ShapeDtypeStruct((ROWS + ROWS // 2, 128), BF16), jax.ShapeDtypeStruct((8, 128), F32)],
        in_specs=[SMEM, VMEM], out_specs=[VMEM] * 2,
        scratch_shapes=[pltpu.VMEM((ROWS, 128), F32)], compiler_params=params(),
        cost_estimate=cost(10**9, 4 * 10**6), name="sorted_targets",
    )(dst, entries)
    return dst, row.reshape(NFAR), tile[0], places, ready


def far_last(dst, row, tile, places, ops, column):
    return pl.pallas_call(
        far_kernel, out_shape=jax.ShapeDtypeStruct((NCOEF, 64), F32),
        in_specs=[SMEM, SMEM, SMEM, VMEM, VMEM, VMEM], out_specs=VMEM,
        scratch_shapes=[pltpu.VMEM((TABLE, 128), F32), pltpu.VMEM((ROWS, 128), F32)],
        compiler_params=params(20), cost_estimate=cost(10**9, 8 * 10**6), name="translate",
    )(row, dst, tile, column, ops, places)


def shards(leaves, counts, send_list, pair_list, multipoles, far_list, trans_ops):
    send = send_list.reshape(64)
    block = first_stage(multipoles)
    outgoing = near_first(leaves, counts, send).reshape(8, 8, 4, 128)
    block, outgoing = lax.optimization_barrier((block, outgoing))
    received = lax.all_to_all(outgoing, "grp", 0, 0, tiled=True).reshape(64, 4, 128)
    block, received = lax.optimization_barrier((block, received))
    own, slot = near_pairs(leaves, counts, pair_list.reshape(2 * PAIRS), received)
    block = spread_out(block, "v", 4).reshape(576, 128)
    block, far_list, trans_ops, own, slot = lax.optimization_barrier((block, far_list, trans_ops, own, slot))
    dst, row, tile, places, ready = far_order(far_list[0])
    trans_ops, ready = lax.optimization_barrier((trans_ops, ready))
    ops = stacked_ops(trans_ops, ready)
    block = spread_out(block, "x", 4)
    block, slot, ops = lax.optimization_barrier((block, slot, ops))
    back = lax.all_to_all(slot.reshape(8, 8, 4, 128), "grp", 0, 0, tiled=True).reshape(64, 4, 128)
    local = far_last(dst, row, tile, places, ops, block.reshape(64 * 36, 128))
    forces = near_last(counts, send, own, back)
    return forces, local


def solution(mesh):
    fine = Mesh(mesh.devices.reshape(8, 4, 4, 8), ("u", "v", "x", "grp"))
    every = ("u", "v", "x", "grp")
    return jax.shard_map(
        shards,
        mesh=fine,
        in_specs=(P(every, None, None), P(every), P(every, None, None), P(every, None, None),
                  P(None, every), P(every, None, None), P()),
        out_specs=(P(every, None, None), P(None, every)),
        check_vma=False,
    )
```
